256 devices in a mesh: dp: 4 (over y_lo, core), row: 8 (over x, y_hi), col: 8 (over z).
Axes of the slice: x: 4, y: 4 (y_hi: 2, y_lo: 2; y = y_hi * 2 + y_lo), z: 8, core: 2. Of those that a mesh axis runs over, the one named last changes fastest.
Arguments:
- inputs: bfloat16 [2048, 6144], P('dp', 'row'), may hold values from -600 to 600
- saved_qkv: bfloat16 [2048, 3, 3072], P('dp', None, 'col'), may hold values from -6 to 6
- saved_up: bfloat16 [2048, 12288], P('dp', 'col'), may hold values from -6 to 6
- cotangent: bfloat16 [2048, 6144], P('dp', 'row'), may hold values from -6 to 6
- weight_qkv: bfloat16 [6144, 3, 3072], P('row', None, 'col'), may hold values from -0.078125 to 0.078125
- weight_up: bfloat16 [6144, 12288], P('row', 'col'), may hold values from -0.078125 to 0.078125
- weight_attn: bfloat16 [3072, 6144], P('col', 'row'), may hold values from -0.109375 to 0.109375
- weight_down: bfloat16 [12288, 6144], P('col', 'row'), may hold values from -0.0546875 to 0.0546875
Outputs:
- grad_inputs: bfloat16 [2048, 6144], P(('dp', 'col'), 'row')
- grad_qkv: bfloat16 [8, 4, 192, 3, 3072], P('row', 'dp', None, None, 'col')
- grad_up: bfloat16 [8, 4, 192, 12288], P('row', 'dp', None, 'col')
- grad_attn: bfloat16 [8, 4, 96, 6144], P('col', 'dp', None, 'row')
- grad_down: bfloat16 [8, 4, 384, 6144], P('col', 'dp', None, 'row')
The draws below stay inside these ranges and needn't reach their ends.
All inputs are finite; a program needn't handle non-finite values.
Results may differ from the reference program's by a relative error of at most 0.0039.
The reference program's roundings to bfloat16 on the way count: a program that leaves them out, or rounds other values in their place, can miss the bound.
Values may be sent and summed in bfloat16 or wider, within the bound.
A program may use at most 128 MiB of HBM per device.

```python
import math
import jax
import jax.numpy as jnp
from jax import lax

D = 6144
H = 24
HD = 128
FF = 12288
S = 256
A = 3072
IMAGES = 8
TOKENS = 2048
D_SUB = 192
A_SUB = 96
F_SUB = 384
N_DP = 4
N_ROW = 8
N_COL = 8


def draw_inputs(key, part):
    keys = jax.random.split(jax.random.fold_in(key, 11), 4)
    columns = jnp.arange(D, dtype=jnp.float32) / D
    spread = jnp.exp(jax.random.uniform(keys[1], (D,), jnp.float32, 0.0, math.log(10.0)))
    base = jax.random.truncated_normal(keys[0], -4.0, 4.0, (TOKENS, D), jnp.float32)
    ramp = jnp.exp(columns * (0.5 * math.log(3.0)))
    rowscale = jnp.exp(jax.random.uniform(keys[3], (TOKENS, 1), jnp.float32, 0.0, math.log(4.0)))
    values = base * spread * ramp * rowscale * 0.25
    return values.astype(jnp.bfloat16)


def steps_of(own_key, dims, pieces, low, largest):
    def one(dim, blocks):
        draws = jax.random.uniform(jax.random.fold_in(jax.random.fold_in(own_key, 6), dim), (blocks,), jnp.float32, low / len(pieces), largest / len(pieces))
        return jnp.repeat(jnp.exp(draws), dims[dim] // blocks).reshape((-1,) + (1,) * (len(dims) - dim - 1))

    loudness = one(*pieces[0])
    for cut in pieces[1:]:
        loudness = loudness * one(*cut)
    return loudness


def bell_draw(stream_key, dims, scale, most, pieces=(), kind=jnp.bfloat16):
    array = scale * jax.random.normal(stream_key, dims, jnp.float32)
    if pieces:
        array = array * steps_of(stream_key, dims, pieces, -0.22, 0.18)
    return jnp.clip(array, -most, most).astype(kind)


def setup_inputs(seed: int = 0) -> dict:
    seeds = jax.random.split(jax.random.key(seed), 9)
    inputs = draw_inputs(jax.random.fold_in(seeds[8], 71), 0)
    saved_qkv = bell_draw(seeds[1], (TOKENS, 3, A), 1.0, 6.0, ((0, 4), (2, 8)))
    saved_up = bell_draw(seeds[2], (TOKENS, FF), 1.0, 6.0, ((0, 4), (1, 8)))
    cotangent = bell_draw(seeds[3], (TOKENS, D), 1.0, 6.0, ((0, 4), (1, 8)))
    weight_qkv = bell_draw(seeds[4], (D, 3, A), D ** -0.5, 0.078125, ((0, 8), (2, 8)))
    weight_up = bell_draw(seeds[5], (D, FF), D ** -0.5, 0.078125, ((0, 8), (1, 8)))
    weight_attn = bell_draw(seeds[6], (A, D), A ** -0.5, 0.109375, ((0, 8), (1, 8)))
    weight_down = bell_draw(seeds[7], (FF, D), FF ** -0.5, 0.0546875, ((0, 8), (1, 8)))
    return dict(inputs=inputs, saved_qkv=saved_qkv, saved_up=saved_up, cotangent=cotangent, weight_qkv=weight_qkv, weight_up=weight_up, weight_attn=weight_attn, weight_down=weight_down)


EPS = 1e-06
SQRT_HALF = 0.7071067811865476
INV_ROOT_TWO_PI = 0.3989422804014327

def gelu_exact(values):
    return 0.5 * values * (1.0 + jax.scipy.special.erf(values * SQRT_HALF))

def gelu_slope(values):
    cumul = 0.5 * (1.0 + jax.scipy.special.erf(values * SQRT_HALF))
    return cumul + values * jnp.exp(-0.5 * values * values) * INV_ROOT_TWO_PI

def head_norm(values):
    average = lax.optimization_barrier(jnp.mean(values, axis=-1, keepdims=True))
    centred = values - average
    inv_std = lax.rsqrt(lax.optimization_barrier(jnp.mean(centred * centred, axis=-1, keepdims=True)) + EPS)
    return (centred * inv_std, inv_std)

def head_norm_back(normed, inv_std, upstream):
    first = lax.optimization_barrier(jnp.mean(upstream, axis=-1, keepdims=True))
    cross = lax.optimization_barrier(jnp.mean(upstream * normed, axis=-1, keepdims=True))
    return inv_std * (upstream - first - normed * cross)

def reference(inputs, saved_qkv, saved_up, cotangent, weight_qkv, weight_up, weight_attn, weight_down):
    f32 = jnp.float32
    bf16 = jnp.bfloat16
    values = inputs.astype(f32)
    average = lax.optimization_barrier(jnp.sum(values, axis=1, keepdims=True)) / D
    second = lax.optimization_barrier(jnp.sum(values * values, axis=1, keepdims=True)) / D
    inv_std = lax.rsqrt(second - average * average + EPS)
    normed = (values - average) * inv_std
    normed_b = normed.astype(bf16)
    qkv5 = saved_qkv.reshape(IMAGES, S, 3, H, HD)
    query = qkv5[:, :, 0]
    keyed = qkv5[:, :, 1]
    valued = qkv5[:, :, 2]
    q_norm, q_inv = head_norm(query.astype(f32))
    k_norm, k_inv = head_norm(keyed.astype(f32))
    qn_b = q_norm.astype(bf16)
    kn_b = k_norm.astype(bf16)
    scale = HD ** (-0.5)
    scores = jnp.einsum('bqhd,bkhd->bhqk', qn_b.astype(f32), kn_b.astype(f32)) * scale
    expo = jnp.exp(scores)
    probs = expo / lax.optimization_barrier(jnp.sum(expo, axis=-1, keepdims=True))
    probs_b = probs.astype(bf16)
    attended = jnp.einsum('bhqk,bkhd->bqhd', probs_b.astype(f32), valued.astype(f32)).astype(bf16)
    attended = attended.reshape(TOKENS, A)
    up_vals = saved_up.astype(f32)
    hidden_b = gelu_exact(up_vals).astype(bf16)
    grad_o = jnp.dot(cotangent, weight_attn.T, preferred_element_type=f32).astype(bf16)
    grad_hidden = jnp.dot(cotangent, weight_down.T, preferred_element_type=f32)
    grad_pre = (grad_hidden * gelu_slope(up_vals)).astype(bf16)
    grad_o4 = grad_o.reshape(IMAGES, S, H, HD)
    grad_probs = jnp.einsum('bqhd,bkhd->bhqk', grad_o4.astype(f32), valued.astype(f32))
    grad_value = jnp.einsum('bhqk,bqhd->bkhd', probs_b.astype(f32), grad_o4.astype(f32)).astype(bf16)
    rowdot = lax.optimization_barrier(jnp.sum(probs * grad_probs, axis=-1, keepdims=True))
    grad_scores = (probs * (grad_probs - rowdot) * scale).astype(bf16)
    grad_qn = jnp.einsum('bhqk,bkhd->bqhd', grad_scores.astype(f32), kn_b.astype(f32))
    grad_kn = jnp.einsum('bhqk,bqhd->bkhd', grad_scores.astype(f32), qn_b.astype(f32))
    grad_query = head_norm_back(q_norm, q_inv, grad_qn).astype(bf16)
    grad_key = head_norm_back(k_norm, k_inv, grad_kn).astype(bf16)
    grad_flat = jnp.stack([grad_query, grad_key, grad_value], axis=2).reshape(TOKENS, 3 * A)
    flat_weight = weight_qkv.reshape(D, 3 * A)
    grad_normed = jnp.dot(grad_flat, flat_weight.T, preferred_element_type=f32)
    grad_normed = grad_normed + jnp.dot(grad_pre, weight_up.T, preferred_element_type=f32)
    mean_grad = lax.optimization_barrier(jnp.sum(grad_normed, axis=1, keepdims=True)) / D
    mean_cross = lax.optimization_barrier(jnp.sum(grad_normed * normed, axis=1, keepdims=True)) / D
    grad_inputs = (cotangent.astype(f32) + inv_std * (grad_normed - mean_grad - normed * mean_cross)).astype(bf16)
    full_qkv = jnp.dot(normed_b.T, grad_flat, preferred_element_type=f32).astype(bf16)
    grad_qkv = full_qkv.reshape(N_ROW, N_DP, D_SUB, 3, A)
    full_up = jnp.dot(normed_b.T, grad_pre, preferred_element_type=f32).astype(bf16)
    grad_up = full_up.reshape(N_ROW, N_DP, D_SUB, FF)
    full_attn = jnp.dot(attended.T, cotangent, preferred_element_type=f32).astype(bf16)
    grad_attn = full_attn.reshape(N_COL, N_DP, A_SUB, D)
    full_down = jnp.dot(hidden_b.T, cotangent, preferred_element_type=f32).astype(bf16)
    grad_down = full_down.reshape(N_COL, N_DP, F_SUB, D)
    return (grad_inputs, grad_qkv, grad_up, grad_attn, grad_down)
```

```python
import jax
import jax.numpy as jnp
from jax import lax
from jax.experimental import pallas as pl
from jax.experimental.pallas import tpu as pltpu
from jax.sharding import PartitionSpec as P

MESH = pl.DeviceIdType.MESH
HD = 128
S = 256
EPS = 1e-06
SQRT_HALF = 0.7071067811865476
INV_ROOT_TWO_PI = 0.3989422804014327
F32 = jnp.float32
BF16 = jnp.bfloat16
N_COPIES = 69


def nt(a, b):
    return lax.dot_general(a, b, (((1,), (1,)), ((), ())), preferred_element_type=F32)


def tn(a, b):
    return lax.dot_general(a, b, (((0,), (0,)), ((), ())), preferred_element_type=F32)


def nn(a, b):
    return lax.dot_general(a, b, (((1,), (0,)), ((), ())), preferred_element_type=F32)


def gelu_exact(values):
    return 0.5 * values * (1.0 + lax.erf(values * SQRT_HALF))


def gelu_slope(values):
    cumul = 0.5 * (1.0 + lax.erf(values * SQRT_HALF))
    return cumul + values * jnp.exp(-0.5 * values * values) * INV_ROOT_TWO_PI


def head_norm(values):
    average = jnp.mean(values, axis=-1, keepdims=True)
    centred = values - average
    inv_std = lax.rsqrt(jnp.mean(centred * centred, axis=-1, keepdims=True) + EPS)
    return (centred * inv_std, inv_std)


def head_norm_back(normed, inv_std, upstream):
    first = jnp.mean(upstream, axis=-1, keepdims=True)
    cross = jnp.mean(upstream * normed, axis=-1, keepdims=True)
    return inv_std * (upstream - first - normed * cross)


def span(start, size):
    return pl.ds(pl.multiple_of(start, size), size)


def kernel(
    inp_h, qkv_h, up_h, cot_h, wqkv_h, wup_h, wattn_h, wdown_h,
    gin_o, gqkv_o, gup_o, gattn_o, gdown_o,
    inp, qkv, up, cot, wqkv, wup, wattn, wdown,
    stat_s, stat_r, stat_y,
    pa, pa_r, pay_s, pay_r,
    ph, phb, ph_r, phy_s, phy_r,
    go, gp, gf, hid, hid_s, att, n_t, n_p, probs_v, qn_v, kn_v,
    tot, zs, zr, fin_s, fin_r, fin_y,
    wgd, wga, wgq, wgu, ysd, yrd, ysa, yra, ysq, yrq, ysu, yru,
    load_sem, send_sem, recv_sem,
):
    dp, row, col = lax.axis_index("dp"), lax.axis_index("row"), lax.axis_index("col")
    y_lo, core = dp // 2, dp % 2
    x, y_hi = row // 2, row % 2
    width = 6144.0
    sib_dev = (y_lo * 2 + (1 - core), row, col)
    ylo_dev = ((1 - y_lo) * 2 + core, row, col)
    yhi_dev = (dp, x * 2 + (1 - y_hi), col)
    x_of = [(x + d) % 4 for d in (1, 2, 3)]
    x_dev = [(dp, xp * 2 + y_hi, col) for xp in x_of]
    z_of = [(col + d) % 8 for d in range(1, 8)]
    z_dev = [(dp, row, zp) for zp in z_of]

    loads = []
    for i, (src, dst) in enumerate([
        (cot_h, cot.at[0]), (wattn_h, wattn), (inp_h, inp), (wdown_h, wdown),
        (qkv_h, qkv), (up_h, up), (wqkv_h, wqkv), (wup_h, wup),
    ]):
        cp = pltpu.make_async_copy(src, dst, load_sem.at[i])
        cp.start()
        loads.append(cp)
    l_cot, l_wattn, l_inp, l_wdown, l_qkv, l_up, l_wqkv, l_wup = loads

    partners = [sib_dev, ylo_dev, yhi_dev] + x_dev + z_dev
    barrier = pltpu.get_barrier_semaphore()
    for dev in partners:
        pl.semaphore_signal(barrier, inc=1, device_id=dev, device_id_type=MESH)
    pl.semaphore_wait(barrier, len(partners))

    sent = []

    def push(src, dst, dev):
        i = len(sent)
        cp = pltpu.make_async_remote_copy(
            src, dst, send_sem.at[i], recv_sem.at[i], device_id=dev, device_id_type=MESH
        )
        cp.start()
        sent.append(cp)
        return cp

    l_inp.wait()
    stat_s[...] = jnp.zeros_like(stat_s)

    for g in range(4):
        block = inp[2 * g : 2 * g + 2].reshape(128, 768).astype(F32)
        block_t = block.T
        lanes = pl.ds(g * 128, 128)
        stat_s[0:1, lanes] = jnp.sum(block_t, axis=0, keepdims=True)
        stat_s[1:2, lanes] = jnp.sum(block_t * block_t, axis=0, keepdims=True)
        n_t[:, lanes] = block_t.astype(BF16)
    c_stat = [push(stat_s, stat_r.at[d], x_dev[d]) for d in range(3)]

    l_cot.wait()
    l_wattn.wait()
    c_cot = push(cot.at[0], cot.at[1], sib_dev)

    @pl.loop(0, 2)
    def _(b):
        acc = nt(cot[0, pl.ds(b * 4, 4)].reshape(256, 768), wattn[...])
        pa[pl.ds(b * 4, 4)] = acc.reshape(4, 2, 32, 384)

    c_pa = [push(pa.at[pl.ds(2 * x_of[d], 2)], pa_r.at[d], x_dev[d]) for d in range(3)]

    l_wdown.wait()
    c_ph = []
    for p in range(2):
        @pl.loop(0, 6)
        def _(n):
            cols = span(n * 256, 256)
            acc = nt(cot[0, :, p].reshape(256, 768), wdown[cols, :]).reshape(8, 32, 256)
            ph[:, p, :, cols] = acc
            phb[:, p, :, cols] = acc.astype(BF16)

        c_ph.append([
            push(phb.at[pl.ds(2 * x_of[d], 2), p], ph_r.at[p, d], x_dev[d]) for d in range(3)
        ])

    l_up.wait()
    for s in range(4):
        @pl.loop(0, 8)
        def _(r):
            hid[s, r] = gelu_exact(up[r, :, :, s * 384 : (s + 1) * 384].astype(F32)).astype(BF16)

    c_hid = [push(hid.at[2 * j + 1 - core], hid_s.at[j], sib_dev) for j in range(2)]

    for cp in c_stat:
        cp.wait_recv()
    stat_y[...] = stat_s[...] + stat_r[0] + stat_r[1] + stat_r[2]
    c_staty = push(stat_y, stat_r.at[3], yhi_dev)

    l_qkv.wait()
    scale = HD ** (-0.5)

    @pl.loop(0, 6)
    def _(i):
        b, h = i // 3, i % 3
        rows = span(b * 256, 256)
        lanes = span(h * 128, 128)
        qn, _ = head_norm(qkv[rows, lanes].astype(F32))
        kn, _ = head_norm(qkv[rows, span(384 + h * 128, 128)].astype(F32))
        qn_b = qn.astype(BF16)
        kn_b = kn.astype(BF16)
        qn_v[rows, lanes] = qn_b
        kn_v[rows, lanes] = kn_b
        expo = jnp.exp(nt(qn_b, kn_b) * scale)
        probs = expo / jnp.sum(expo, axis=-1, keepdims=True)
        probs_v[i] = probs
        att[0, rows, lanes] = nn(
            probs.astype(BF16), qkv[rows, span(768 + h * 128, 128)]
        ).astype(BF16)

    c_att = push(att.at[0], att.at[1], sib_dev)

    own = x * 2 + y_hi
    other = x * 2 + (1 - y_hi)
    for cp in c_pa:
        cp.wait_recv()
    pay_s[...] = pa[other] + pa_r[0, 1 - y_hi] + pa_r[1, 1 - y_hi] + pa_r[2, 1 - y_hi]
    c_pay = push(pay_s, pay_r, yhi_dev)
    part_o = pa[own] + pa_r[0, y_hi] + pa_r[1, y_hi] + pa_r[2, y_hi]

    c_staty.wait_recv()
    stat = stat_y[...] + stat_r[3]
    mean_r = stat[0:1] / width
    inv_r = lax.rsqrt(stat[1:2] / width - mean_r * mean_r + EPS)

    @pl.loop(0, 8)
    def _(k):
        rows = span(k * 96, 96)
        n_t[rows, :] = ((n_t[rows, :].astype(F32) - mean_r) * inv_r).astype(BF16)

    c_nt = [
        push(n_t.at[span((2 * j + 1 - core) * 192, 192)], n_p.at[j, :, pl.ds(512, 512)], sib_dev)
        for j in range(2)
    ]
    l_nt = []
    for j in range(2):
        cp = pltpu.make_async_copy(
            n_t.at[span((2 * j + core) * 192, 192)], n_p.at[j, :, pl.ds(0, 512)], load_sem.at[8 + j]
        )
        cp.start()
        l_nt.append(cp)

    c_pay.wait_recv()
    go[own] = (part_o + pay_r[...]).astype(BF16)
    c_goy = push(go.at[own], go.at[own], yhi_dev)
    c_go = [push(go.at[own], go.at[own], dev) for dev in x_dev]

    def hidden_sum(p):
        for cp in c_ph[p]:
            cp.wait_recv()
        o = 1 - y_hi
        phy_s[p] = (
            ph[other, p] + ph_r[p, 0, o].astype(F32) + ph_r[p, 1, o].astype(F32)
            + ph_r[p, 2, o].astype(F32)
        )
        return push(phy_s.at[p], phy_r.at[p], yhi_dev)

    def hidden_slope(p, cp):
        part = (
            ph[own, p] + ph_r[p, 0, y_hi].astype(F32) + ph_r[p, 1, y_hi].astype(F32)
            + ph_r[p, 2, y_hi].astype(F32)
        )
        slope = gelu_slope(up[own, p].astype(F32))
        cp.wait_recv()
        gp[0, own, p] = ((part + phy_r[p]) * slope).astype(BF16)
        here = gp.at[0, own, p]
        return push(here, here, yhi_dev), [push(here, here, dev) for dev in x_dev]

    def relay(cp, ref):
        cp.wait_recv()
        return [push(ref, ref, dev) for dev in x_dev]

    c_cot.wait_recv()
    for cp in c_hid:
        cp.wait_recv()
    y_other = 1 - y_lo

    def down(j):
        @pl.loop(0, 3)
        def _(n):
            cols = span(n * 256, 256)
            acc = tn(hid[2 * j + core].reshape(512, 384), cot[0, :, :, :, cols].reshape(512, 256))
            acc += tn(hid_s[j].reshape(512, 384), cot[1, :, :, :, cols].reshape(512, 256))
            wgd[j, :, cols] = acc

    down(y_other)
    ysd[...] = wgd[y_other].astype(BF16)
    c_d = push(ysd, yrd, ylo_dev)
    c_phy0 = hidden_sum(0)
    c_gof = relay(c_goy, go.at[other])
    down(y_lo)
    c_gpy0, c_gp0 = hidden_slope(0, c_phy0)

    c_att.wait_recv()

    @pl.loop(0, 3)
    def _(n):
        cols = span(n * 256, 256)
        acc = tn(att[0], cot[0, :, :, :, cols].reshape(512, 256))
        acc += tn(att[1], cot[1, :, :, :, cols].reshape(512, 256))
        wga[:, cols] = acc

    ysa[...] = wga[span((2 * y_other + core) * 96, 96), :].astype(BF16)
    c_a = push(ysa, yra, ylo_dev)

    c_gpf0 = relay(c_gpy0, gp.at[0, other, 0])
    c_phy1 = hidden_sum(1)

    for cp in c_go + c_gof:
        cp.wait_recv()

    @pl.loop(0, 6)
    def _(i):
        b, h = i // 3, i % 3
        rows = span(b * 256, 256)
        lanes = span(h * 128, 128)
        lanes_k = span(384 + h * 128, 128)
        lanes_v = span(768 + h * 128, 128)
        grad_o = go[pl.ds(b * 4, 4), :, :, lanes].reshape(256, 128)
        probs = probs_v[i]
        probs_b = probs.astype(BF16)
        grad_probs = nt(grad_o, qkv[rows, lanes_v])
        gf[0, rows, lanes_v] = tn(probs_b, grad_o).astype(BF16)
        rowdot = jnp.sum(probs * grad_probs, axis=-1, keepdims=True)
        grad_scores = (probs * (grad_probs - rowdot) * scale).astype(BF16)
        q_norm, q_inv = head_norm(qkv[rows, lanes].astype(F32))
        grad_qn = nn(grad_scores, kn_v[rows, lanes])
        gf[0, rows, lanes] = head_norm_back(q_norm, q_inv, grad_qn).astype(BF16)
        k_norm, k_inv = head_norm(qkv[rows, lanes_k].astype(F32))
        grad_kn = tn(grad_scores, qn_v[rows, lanes])
        gf[0, rows, lanes_k] = head_norm_back(k_norm, k_inv, grad_kn).astype(BF16)

    c_gf = push(gf.at[0], gf.at[1], sib_dev)
    c_gpy1, c_gp1 = hidden_slope(1, c_phy1)

    l_wqkv.wait()

    @pl.loop(0, 6)
    def _(i):
        b, n = i // 3, i % 3
        cols = span(n * 256, 256)
        acc = nt(gf[0, span(b * 256, 256), :], wqkv[cols, :])
        tot[pl.ds(b * 4, 4), :, :, cols] = acc.reshape(4, 2, 32, 256)

    c_gpf1 = relay(c_gpy1, gp.at[0, other, 1])

    c_gf.wait_recv()
    for cp in c_nt:
        cp.wait_recv()
    for cp in l_nt:
        cp.wait()

    @pl.loop(0, 3)
    def _(n):
        cols = span(n * 384, 384)
        acc = nn(n_p[...].reshape(384, 1024), gf[:, :, cols].reshape(1024, 384))
        wgq[:, :, cols] = acc.reshape(2, 192, 384)

    ysq[...] = wgq[y_other].astype(BF16)
    c_q = push(ysq, yrq, ylo_dev)

    l_wup.wait()
    c_z = []
    c_gps = []
    for p, waits in ((0, c_gp0 + c_gpf0), (1, c_gp1 + c_gpf1)):
        for cp in waits:
            cp.wait_recv()
        c_gps.append(push(gp.at[0, :, p], gp.at[1, :, p], sib_dev))

        @pl.loop(0, 3)
        def _(n):
            cols = span(n * 256, 256)
            acc = nt(gp[0, :, p].reshape(256, 1536), wup[cols, :]).reshape(8, 32, 256)
            acc = acc + tot[:, p, :, cols]
            tot[:, p, :, cols] = acc
            zs[p, :, :, cols] = acc.astype(BF16)

        c_z.append([push(zs.at[p, z_of[d]], zr.at[p, d], z_dev[d]) for d in range(7)])

    for cp in c_gps:
        cp.wait_recv()
    c_u = []
    for half in range(2):
        @pl.loop(0, 3)
        def _(n):
            cols = span(half * 768 + n * 256, 256)
            acc = nn(n_p[...].reshape(384, 1024), gp[:, :, :, :, cols].reshape(1024, 256))
            wgu[half, :, :, span(n * 256, 256)] = acc.reshape(2, 192, 256)

        ysu[half] = wgu[half, y_other].astype(BF16)
        c_u.append(push(ysu.at[half], yru.at[half], ylo_dev))

    lane = lax.broadcasted_iota(jnp.int32, (64, 512), 1)
    token = lax.broadcasted_iota(jnp.int32, (64, 512), 0)
    pick = jnp.where(lane == token + col * 64, 1.0, 0.0).astype(F32)
    mean_c = jnp.sum(pick * mean_r, axis=1, keepdims=True)
    inv_c = jnp.sum(pick * inv_r, axis=1, keepdims=True)
    normed = (inp[col].reshape(64, 768).astype(F32) - mean_c) * inv_c
    gn = []
    for p in range(2):
        for cp in c_z[p]:
            cp.wait_recv()
        value = tot[col, p]
        for d in range(7):
            value = value + zr[p, d].astype(F32)
        gn.append(value)
    grad_n = jnp.concatenate(gn, axis=0)
    sum_g = jnp.sum(grad_n, axis=1, keepdims=True)
    sum_c = jnp.sum(grad_n * normed, axis=1, keepdims=True)
    lane = lax.broadcasted_iota(jnp.int32, (64, 128), 1)
    token = lax.broadcasted_iota(jnp.int32, (64, 128), 0)
    eye = jnp.where(lane == token, 1.0, 0.0).astype(F32)
    fin_s[...] = jnp.zeros_like(fin_s)
    fin_s[0:1, :] = jnp.sum(eye * sum_g, axis=0, keepdims=True)
    fin_s[1:2, :] = jnp.sum(eye * sum_c, axis=0, keepdims=True)
    c_fin = [push(fin_s, fin_r.at[d], x_dev[d]) for d in range(3)]

    c_d.wait_recv()
    gdown_o[...] = (wgd[y_lo] + yrd[...].astype(F32)).astype(BF16)
    c_a.wait_recv()
    gattn_o[...] = (
        wga[span((2 * y_lo + core) * 96, 96), :] + yra[...].astype(F32)
    ).astype(BF16)

    for cp in c_fin:
        cp.wait_recv()
    fin_y[...] = fin_s[...] + fin_r[0] + fin_r[1] + fin_r[2]
    c_finy = push(fin_y, fin_r.at[3], yhi_dev)

    c_q.wait_recv()
    gqkv_o[...] = (wgq[y_lo] + yrq[...].astype(F32)).astype(BF16)

    c_finy.wait_recv()
    fin = fin_y[...] + fin_r[3]
    mean_g = jnp.sum(eye * fin[0:1], axis=1, keepdims=True) / width
    mean_x = jnp.sum(eye * fin[1:2], axis=1, keepdims=True) / width
    branch = grad_n - mean_g - normed * mean_x
    result = cot[0, col].reshape(64, 768).astype(F32) + inv_c * branch
    gin_o[...] = result.astype(BF16)

    for half in range(2):
        c_u[half].wait_recv()
        gup_o[:, half * 768 : (half + 1) * 768] = (
            wgu[half, y_lo] + yru[half].astype(F32)
        ).astype(BF16)

    for cp in sent:
        cp.wait_send()
    assert len(sent) == N_COPIES, len(sent)


def body(inputs, saved_qkv, saved_up, cotangent, weight_qkv, weight_up, weight_attn, weight_down):
    vm = pltpu.VMEM
    scratch = [
        vm((8, 2, 32, 768), BF16), vm((512, 1152), BF16), vm((8, 2, 32, 1536), BF16),
        vm((2, 8, 2, 32, 768), BF16),
        vm((768, 1152), BF16), vm((768, 1536), BF16), vm((384, 768), BF16), vm((1536, 768), BF16),
        vm((8, 512), F32), vm((4, 8, 512), F32), vm((8, 512), F32),
        vm((8, 2, 32, 384), F32), vm((3, 2, 2, 32, 384), F32),
        vm((2, 32, 384), F32), vm((2, 32, 384), F32),
        vm((8, 2, 32, 1536), F32), vm((8, 2, 32, 1536), BF16), vm((2, 3, 2, 32, 1536), BF16),
        vm((2, 32, 1536), F32), vm((2, 32, 1536), F32),
        vm((8, 2, 32, 384), BF16), vm((2, 8, 2, 32, 1536), BF16), vm((2, 512, 1152), BF16),
        vm((4, 8, 2, 32, 384), BF16), vm((2, 8, 2, 32, 384), BF16), vm((2, 512, 384), BF16),
        vm((768, 512), BF16), vm((2, 192, 1024), BF16),
        vm((6, 256, 256), F32), vm((512, 384), BF16), vm((512, 384), BF16),
        vm((8, 2, 32, 768), F32), vm((2, 8, 32, 768), BF16), vm((2, 7, 32, 768), BF16),
        vm((8, 128), F32), vm((4, 8, 128), F32), vm((8, 128), F32),
        vm((2, 384, 768), F32), vm((384, 768), F32), vm((2, 192, 1152), F32),
        vm((2, 2, 192, 768), F32),
        vm((384, 768), BF16), vm((384, 768), BF16), vm((96, 768), BF16), vm((96, 768), BF16),
        vm((192, 1152), BF16), vm((192, 1152), BF16),
        vm((2, 192, 768), BF16), vm((2, 192, 768), BF16),
        pltpu.SemaphoreType.DMA((10,)),
        pltpu.SemaphoreType.DMA((N_COPIES,)),
        pltpu.SemaphoreType.DMA((N_COPIES,)),
    ]
    gin, gqkv, gup, gattn, gdown = pl.pallas_call(
        kernel,
        out_shape=(
            jax.ShapeDtypeStruct((64, 768), BF16),
            jax.ShapeDtypeStruct((192, 1152), BF16),
            jax.ShapeDtypeStruct((192, 1536), BF16),
            jax.ShapeDtypeStruct((96, 768), BF16),
            jax.ShapeDtypeStruct((384, 768), BF16),
        ),
        in_specs=[pl.BlockSpec(memory_space=pl.ANY)] * 8,
        out_specs=[pl.BlockSpec(memory_space=pltpu.VMEM)] * 5,
        scratch_shapes=scratch,
        compiler_params=pltpu.CompilerParams(
            collective_id=0, has_side_effects=True, vmem_limit_bytes=58 * 2**20
        ),
        name="layer_backward",
    )(
        inputs.reshape(8, 2, 32, 768),
        saved_qkv.reshape(512, 1152),
        saved_up.reshape(8, 2, 32, 1536),
        cotangent.reshape(8, 2, 32, 768),
        weight_qkv.reshape(768, 1152),
        weight_up,
        weight_attn,
        weight_down,
    )
    return (
        gin,
        gqkv.reshape(1, 1, 192, 3, 384),
        gup.reshape(1, 1, 192, 1536),
        gattn.reshape(1, 1, 96, 768),
        gdown.reshape(1, 1, 384, 768),
    )


def solution(mesh):
    return jax.shard_map(
        body,
        mesh=mesh,
        in_specs=(
            P("dp", "row"),
            P("dp", None, "col"),
            P("dp", "col"),
            P("dp", "row"),
            P("row", None, "col"),
            P("row", "col"),
            P("col", "row"),
            P("col", "row"),
        ),
        out_specs=(
            P(("dp", "col"), "row"),
            P("row", "dp", None, None, "col"),
            P("row", "dp", None, "col"),
            P("col", "dp", None, "row"),
            P("col", "dp", None, "row"),
        ),
        check_vma=False,
    )
```

```python
import jax
import jax.numpy as jnp
from jax import lax
from jax.experimental import pallas as pl
from jax.experimental.pallas import tpu as pltpu
from jax.sharding import PartitionSpec as P

MESH = pl.DeviceIdType.MESH
HD = 128
S = 256
EPS = 1e-06
SQRT_HALF = 0.7071067811865476
INV_ROOT_TWO_PI = 0.3989422804014327
F32 = jnp.float32
BF16 = jnp.bfloat16
N_COPIES = 85


def nt(a, b):
    return lax.dot_general(a, b, (((1,), (1,)), ((), ())), preferred_element_type=F32)


def tn(a, b):
    return lax.dot_general(a, b, (((0,), (0,)), ((), ())), preferred_element_type=F32)


def nn(a, b):
    return lax.dot_general(a, b, (((1,), (0,)), ((), ())), preferred_element_type=F32)


def gelu_exact(values):
    return 0.5 * values * (1.0 + lax.erf(values * SQRT_HALF))


def gelu_slope(values):
    cumul = 0.5 * (1.0 + lax.erf(values * SQRT_HALF))
    return cumul + values * jnp.exp(-0.5 * values * values) * INV_ROOT_TWO_PI


def head_norm(values):
    average = jnp.mean(values, axis=-1, keepdims=True)
    centred = values - average
    inv_std = lax.rsqrt(jnp.mean(centred * centred, axis=-1, keepdims=True) + EPS)
    return (centred * inv_std, inv_std)


def head_norm_back(normed, inv_std, upstream):
    first = jnp.mean(upstream, axis=-1, keepdims=True)
    cross = jnp.mean(upstream * normed, axis=-1, keepdims=True)
    return inv_std * (upstream - first - normed * cross)


def span(start, size):
    return pl.ds(pl.multiple_of(start, size), size)


def kernel(
    inp_h, qkv_h, up_h, cot_h, wqkv_h, wup_h, wattn_h, wdown_h,
    gin_o, gqkv_o, gup_o, gattn_o, gdown_o,
    inp, qkv, up, cot, wqkv, wup, wattn, wdown,
    stat_s, stat_r, stat_y,
    pa, pa_r, pay_s, pay_r,
    ph, phb, ph_r, phx, phy_s, phy_r,
    go, gp, gf, hid, hid_s, att, n_t, n_p, probs_v, qn_v, kn_v,
    tot, zs, zr, fin_s, fin_r, fin_y,
    wgd, wga, wgq, wgu, ysd, yrd, ysa, yra, ysq, yrq, ysu, yru,
    load_sem, send_sem, recv_sem,
):
    dp, row, col = lax.axis_index("dp"), lax.axis_index("row"), lax.axis_index("col")
    y_lo, core = dp // 2, dp % 2
    x, y_hi = row // 2, row % 2
    y_other = 1 - y_lo
    width = 6144.0
    scale = HD ** (-0.5)
    x_next, x_far, x_prev = (x + 1) % 4, (x + 2) % 4, (x + 3) % 4
    sib_dev = (y_lo * 2 + (1 - core), row, col)
    ylo_dev = (y_other * 2 + core, row, col)
    yhi_dev = (dp, x * 2 + (1 - y_hi), col)
    next_dev = (dp, x_next * 2 + y_hi, col)
    far_dev = (dp, x_far * 2 + y_hi, col)
    prev_dev = (dp, x_prev * 2 + y_hi, col)
    x_dev = [next_dev, far_dev, prev_dev]
    z_of = [(col + d) % 8 for d in range(1, 8)]
    z_dev = [(dp, row, zp) for zp in z_of]

    def load(i, src, dst):
        cp = pltpu.make_async_copy(src, dst, load_sem.at[i])
        cp.start()
        return cp

    l_cot = load(0, cot_h, cot.at[0])
    l_wattn = load(1, wattn_h, wattn)

    partners = [sib_dev, ylo_dev, yhi_dev] + x_dev + z_dev
    barrier = pltpu.get_barrier_semaphore()
    for dev in partners:
        pl.semaphore_signal(barrier, inc=1, device_id=dev, device_id_type=MESH)

    sent = []

    def push(src, dst, dev):
        i = len(sent)
        cp = pltpu.make_async_remote_copy(
            src, dst, send_sem.at[i], recv_sem.at[i], device_id=dev, device_id_type=MESH
        )
        cp.start()
        sent.append(cp)
        return cp

    x_of = [x_next, x_far, x_prev]

    def scatter(block, land):
        return [push(block(x_of[d]), land.at[d], x_dev[d]) for d in range(3)]

    def gather(chunk):
        cps = []
        for dev in (next_dev, prev_dev):
            for i in range(2):
                ref = chunk(2 * x + i)
                cps.append(push(ref, ref, dev))
        return cps

    def gather_far(chunk, cps):
        cps[0].wait_recv()
        ref = chunk(2 * x_prev)
        cps.append(push(ref, ref, next_dev))
        cps[3].wait_recv()
        ref = chunk(2 * x_next + 1)
        cps.append(push(ref, ref, prev_dev))

    def gather_end(cps):
        for i in (1, 2, 4, 5):
            cps[i].wait_recv()

    l_cot.wait()
    l_wattn.wait()

    @pl.loop(0, 2)
    def _(b):
        acc = nt(cot[0, pl.ds(b * 4, 4)].reshape(256, 768), wattn[...])
        pa[pl.ds(b * 4, 4)] = acc.reshape(4, 2, 32, 384)

    l_up = load(2, up_h, up)
    l_wdown = load(3, wdown_h, wdown)
    l_qkv = load(4, qkv_h, qkv)
    l_inp = load(5, inp_h, inp)

    def activate(y):
        @pl.loop(0, 16)
        def _(i):
            r, s = i // 2, 2 * y + i % 2
            hid[s, r] = gelu_exact(up[r, :, :, span(s * 384, 384)].astype(F32)).astype(BF16)

    pl.semaphore_wait(barrier, len(partners))
    c_pa = scatter(lambda xp: pa.at[pl.ds(2 * xp, 2)], pa_r)
    c_cot = push(cot.at[0], cot.at[1], sib_dev)
    l_up.wait()
    activate(y_other)
    c_hid = [push(hid.at[2 * y_other + 1 - core], hid_s.at[y_other], sib_dev)]
    l_wdown.wait()
    l_wqkv = load(6, wqkv_h, wqkv)
    l_wup = load(7, wup_h, wup)

    def hidden_start(c, p):
        @pl.loop(0, 3)
        def _(n):
            cols = span(n * 256, 256)
            acc = nt(
                cot[0, :, p].reshape(256, 768), wdown[span(c * 768 + n * 256, 256), :]
            ).reshape(8, 32, 256)
            ph[c, :, p, :, cols] = acc
            phb[c, :, p, :, cols] = acc.astype(BF16)

        return scatter(lambda xp: phb.at[c, pl.ds(2 * xp, 2), p], ph_r.at[c, p])

    def hidden_sum(c, p, cps):
        for cp in cps:
            cp.wait_recv()
        total = ph[c, pl.ds(2 * x, 2), p]
        for d in range(3):
            total = total + ph_r[c, p, d].astype(F32)
        phx[c, p] = total
        phy_s[c, p] = total.astype(BF16)
        return push(phy_s.at[c, p], phy_r.at[c, p], yhi_dev)

    def hidden_chunk(c, p):
        return lambda r: gp.at[0, c, r, p]

    def hidden_slope(c, p, cp):
        slope = gelu_slope(up[pl.ds(2 * x, 2), p, :, c * 768 : (c + 1) * 768].astype(F32))
        cp.wait_recv()
        gp[0, c, pl.ds(2 * x, 2), p] = (
            (phx[c, p] + phy_r[c, p].astype(F32)) * slope
        ).astype(BF16)
        return gather(hidden_chunk(c, p))

    def down(j):
        @pl.loop(0, 3)
        def _(n):
            cols = span(n * 256, 256)
            acc = tn(hid[2 * j + core].reshape(512, 384), cot[0, :, :, :, cols].reshape(512, 256))
            acc += tn(hid_s[j].reshape(512, 384), cot[1, :, :, :, cols].reshape(512, 256))
            wgd[j, :, cols] = acc

    def attention(b):
        @pl.loop(0, 3)
        def _(h):
            rows = pl.ds(b * 256, 256)
            lanes = span(h * 128, 128)
            qn, _ = head_norm(qkv[0, rows, lanes].astype(F32))
            kn, _ = head_norm(qkv[1, rows, lanes].astype(F32))
            qn_b = qn.astype(BF16)
            kn_b = kn.astype(BF16)
            qn_v[rows, lanes] = qn_b
            kn_v[rows, lanes] = kn_b
            expo = jnp.exp(nt(qn_b, kn_b) * scale)
            probs = expo / jnp.sum(expo, axis=-1, keepdims=True)
            probs_v[b * 3 + h] = probs
            att[0, rows, lanes] = nn(probs.astype(BF16), qkv[2, rows, lanes]).astype(BF16)

    def attention_back(b):
        @pl.loop(0, 3)
        def _(h):
            rows = pl.ds(b * 256, 256)
            lanes = span(h * 128, 128)
            grad_o = go[pl.ds(b * 4, 4), :, :, lanes].reshape(256, 128)
            probs = probs_v[b * 3 + h]
            probs_b = probs.astype(BF16)
            grad_probs = nt(grad_o, qkv[2, rows, lanes])
            gf[0, 2, rows, lanes] = tn(probs_b, grad_o).astype(BF16)
            rowdot = jnp.sum(probs * grad_probs, axis=-1, keepdims=True)
            grad_scores = (probs * (grad_probs - rowdot) * scale).astype(BF16)
            q_norm, q_inv = head_norm(qkv[0, rows, lanes].astype(F32))
            grad_qn = nn(grad_scores, kn_v[rows, lanes])
            gf[0, 0, rows, lanes] = head_norm_back(q_norm, q_inv, grad_qn).astype(BF16)
            k_norm, k_inv = head_norm(qkv[1, rows, lanes].astype(F32))
            grad_kn = tn(grad_scores, qn_v[rows, lanes])
            gf[0, 1, rows, lanes] = head_norm_back(k_norm, k_inv, grad_kn).astype(BF16)

    def share(c, p):
        gather_end(c_gp[c, p])
        return push(gp.at[0, c, :, p], gp.at[1, c, :, p], sib_dev)

    c_ph = {}
    c_ph[0, 0] = hidden_start(0, 0)

    c_cot.wait_recv()
    c_hid[0].wait_recv()
    down(y_other)
    ysd[...] = wgd[y_other].astype(BF16)
    c_d = push(ysd, yrd, ylo_dev)

    c_ph[0, 1] = hidden_start(0, 1)
    c_ph[1, 0] = hidden_start(1, 0)
    c_ph[1, 1] = hidden_start(1, 1)

    l_qkv.wait()
    attention(0)

    mine = pl.ds(2 * x, 2)
    for cp in c_pa:
        cp.wait_recv()
    pay_s[...] = pa[mine] + pa_r[0] + pa_r[1] + pa_r[2]
    c_pay = push(pay_s, pay_r, yhi_dev)

    attention(1)
    c_att = push(att.at[0], att.at[1], sib_dev)

    l_inp.wait()
    stat_s[...] = jnp.zeros_like(stat_s)
    for g in range(4):
        block_t = inp[2 * g : 2 * g + 2].reshape(128, 768).astype(F32).T
        lanes = pl.ds(g * 128, 128)
        stat_s[0:1, lanes] = jnp.sum(block_t, axis=0, keepdims=True)
        stat_s[1:2, lanes] = jnp.sum(block_t * block_t, axis=0, keepdims=True)
        n_t[:, lanes] = block_t.astype(BF16)
    c_stat = [push(stat_s, stat_r.at[d], x_dev[d]) for d in range(3)]

    c_att.wait_recv()

    @pl.loop(0, 3)
    def _(n):
        cols = span(n * 256, 256)
        acc = tn(att[0], cot[0, :, :, :, cols].reshape(512, 256))
        acc += tn(att[1], cot[1, :, :, :, cols].reshape(512, 256))
        wga[:, cols] = acc

    ysa[...] = wga[span((2 * y_other + core) * 96, 96), :].astype(BF16)
    c_a = push(ysa, yra, ylo_dev)

    c_pay.wait_recv()
    go[mine] = (pay_s[...] + pay_r[...]).astype(BF16)
    c_go = [push(go.at[mine], go.at[mine], dev) for dev in x_dev]
    c_phy = {(0, 0): hidden_sum(0, 0, c_ph[0, 0])}
    c_phy[0, 1] = hidden_sum(0, 1, c_ph[0, 1])

    for cp in c_stat:
        cp.wait_recv()
    stat_y[...] = stat_s[...] + stat_r[0] + stat_r[1] + stat_r[2]
    c_staty = push(stat_y, stat_r.at[3], yhi_dev)

    c_gp = {(0, 0): hidden_slope(0, 0, c_phy[0, 0])}
    c_phy[1, 0] = hidden_sum(1, 0, c_ph[1, 0])
    c_gp[0, 1] = hidden_slope(0, 1, c_phy[0, 1])
    c_phy[1, 1] = hidden_sum(1, 1, c_ph[1, 1])

    c_staty.wait_recv()
    stat = stat_y[...] + stat_r[3]
    mean_r = stat[0:1] / width
    inv_r = lax.rsqrt(stat[1:2] / width - mean_r * mean_r + EPS)

    @pl.loop(0, 8)
    def _(k):
        rows = span(k * 96, 96)
        n_t[rows, :] = ((n_t[rows, :].astype(F32) - mean_r) * inv_r).astype(BF16)

    c_nt = [
        push(n_t.at[span((2 * j + 1 - core) * 192, 192)], n_p.at[j, :, pl.ds(512, 512)], sib_dev)
        for j in range(2)
    ]
    l_nt = []
    for j in range(2):
        cp = pltpu.make_async_copy(
            n_t.at[span((2 * j + core) * 192, 192)], n_p.at[j, :, pl.ds(0, 512)], load_sem.at[8 + j]
        )
        cp.start()
        l_nt.append(cp)

    for cp in c_go:
        cp.wait_recv()
    attention_back(0)
    c_gp[1, 0] = hidden_slope(1, 0, c_phy[1, 0])
    gather_far(hidden_chunk(0, 0), c_gp[0, 0])
    c_gp[1, 1] = hidden_slope(1, 1, c_phy[1, 1])
    gather_far(hidden_chunk(0, 1), c_gp[0, 1])
    attention_back(1)
    c_gf = push(gf.at[0], gf.at[1], sib_dev)
    for cp in c_nt:
        cp.wait_recv()
    for cp in l_nt:
        cp.wait()
    gather_far(hidden_chunk(1, 0), c_gp[1, 0])
    c_gf.wait_recv()

    @pl.loop(0, 3)
    def _(n):
        acc = nn(n_p[...].reshape(384, 1024), gf[:, n].reshape(1024, 384))
        wgq[:, n] = acc.reshape(2, 192, 384)

    ysq[...] = wgq[y_other].astype(BF16)
    c_q = push(ysq, yrq, ylo_dev)

    gather_far(hidden_chunk(1, 1), c_gp[1, 1])
    c_gps = [share(0, 0), share(0, 1)]

    l_wqkv.wait()
    l_wup.wait()

    @pl.loop(0, 6)
    def _(i):
        b, n = i // 3, i % 3
        cols = span(n * 256, 256)
        rows = span(b * 256, 256)
        acc = nt(gf[0, 0, rows, :], wqkv[0, cols, :])
        acc += nt(gf[0, 1, rows, :], wqkv[1, cols, :])
        acc += nt(gf[0, 2, rows, :], wqkv[2, cols, :])
        tot[pl.ds(b * 4, 4), :, :, cols] = acc.reshape(4, 2, 32, 256)

    def grad_up(c):
        @pl.loop(0, 3)
        def _(n):
            cols = span(n * 256, 256)
            acc = nn(n_p[...].reshape(384, 1024), gp[:, c, :, :, :, cols].reshape(1024, 256))
            wgu[c, :, :, cols] = acc.reshape(2, 192, 256)

        ysu[c] = wgu[c, y_other].astype(BF16)
        return push(ysu.at[c], yru.at[c], ylo_dev)

    for cp in c_gps:
        cp.wait_recv()
    c_u = [grad_up(0)]

    c_z = []
    c_gps = []
    for p in range(2):
        c_gps.append(share(1, p))

        @pl.loop(0, 3)
        def _(n):
            cols = span(n * 256, 256)
            acc = nt(gp[0, 0, :, p].reshape(256, 768), wup[cols, 0:768])
            acc += nt(gp[0, 1, :, p].reshape(256, 768), wup[cols, 768:1536])
            acc = acc.reshape(8, 32, 256) + tot[:, p, :, cols]
            tot[:, p, :, cols] = acc
            zs[p, :, :, cols] = acc.astype(BF16)

        c_z.append([push(zs.at[p, z_of[d]], zr.at[p, d], z_dev[d]) for d in range(7)])

    for cp in c_gps:
        cp.wait_recv()
    c_u.append(grad_up(1))
    activate(y_lo)
    c_hid.append(push(hid.at[2 * y_lo + 1 - core], hid_s.at[y_lo], sib_dev))
    c_hid[1].wait_recv()
    down(y_lo)

    lane = lax.broadcasted_iota(jnp.int32, (64, 512), 1)
    token = lax.broadcasted_iota(jnp.int32, (64, 512), 0)
    pick = jnp.where(lane == token + col * 64, 1.0, 0.0).astype(F32)
    mean_c = jnp.sum(pick * mean_r, axis=1, keepdims=True)
    inv_c = jnp.sum(pick * inv_r, axis=1, keepdims=True)
    normed = (inp[col].reshape(64, 768).astype(F32) - mean_c) * inv_c
    gn = []
    for p in range(2):
        for cp in c_z[p]:
            cp.wait_recv()
        value = tot[col, p]
        for d in range(7):
            value = value + zr[p, d].astype(F32)
        gn.append(value)
    grad_n = jnp.concatenate(gn, axis=0)
    sum_g = jnp.sum(grad_n, axis=1, keepdims=True)
    sum_c = jnp.sum(grad_n * normed, axis=1, keepdims=True)
    lane = lax.broadcasted_iota(jnp.int32, (64, 128), 1)
    token = lax.broadcasted_iota(jnp.int32, (64, 128), 0)
    eye = jnp.where(lane == token, 1.0, 0.0).astype(F32)
    fin_s[...] = jnp.zeros_like(fin_s)
    fin_s[0:1, :] = jnp.sum(eye * sum_g, axis=0, keepdims=True)
    fin_s[1:2, :] = jnp.sum(eye * sum_c, axis=0, keepdims=True)
    c_fin = [push(fin_s, fin_r.at[d], x_dev[d]) for d in range(3)]

    c_d.wait_recv()
    gdown_o[...] = (wgd[y_lo] + yrd[...].astype(F32)).astype(BF16)
    c_a.wait_recv()
    gattn_o[...] = (
        wga[span((2 * y_lo + core) * 96, 96), :] + yra[...].astype(F32)
    ).astype(BF16)

    for cp in c_fin:
        cp.wait_recv()
    fin_y[...] = fin_s[...] + fin_r[0] + fin_r[1] + fin_r[2]
    c_finy = push(fin_y, fin_r.at[3], yhi_dev)

    c_q.wait_recv()
    gqkv_o[...] = (wgq[y_lo] + yrq[...].astype(F32)).astype(BF16)

    c_finy.wait_recv()
    fin = fin_y[...] + fin_r[3]
    mean_g = jnp.sum(eye * fin[0:1], axis=1, keepdims=True) / width
    mean_x = jnp.sum(eye * fin[1:2], axis=1, keepdims=True) / width
    branch = grad_n - mean_g - normed * mean_x
    result = cot[0, col].reshape(64, 768).astype(F32) + inv_c * branch
    gin_o[...] = result.astype(BF16)

    for c in range(2):
        c_u[c].wait_recv()
        gup_o[:, c * 768 : (c + 1) * 768] = (
            wgu[c, y_lo] + yru[c].astype(F32)
        ).astype(BF16)

    for cp in sent:
        cp.wait_send()
    assert len(sent) == N_COPIES, len(sent)


def hand_over(*refs):
    sem = refs[15]
    copies_in = [pltpu.make_async_copy(refs[i], refs[10 + i], sem.at[i]) for i in range(5)]
    copies_out = [pltpu.make_async_copy(refs[10 + i], refs[5 + i], sem.at[5 + i]) for i in range(5)]
    for cp in copies_in:
        cp.start()
    for first, second in zip(copies_in, copies_out):
        first.wait()
        second.start()
    for cp in copies_out:
        cp.wait()


def body(inputs, saved_qkv, saved_up, cotangent, weight_qkv, weight_up, weight_attn, weight_down):
    vm = pltpu.VMEM
    scratch = [
        vm((8, 2, 32, 768), BF16), vm((3, 512, 384), BF16), vm((8, 2, 32, 1536), BF16),
        vm((2, 8, 2, 32, 768), BF16),
        vm((3, 768, 384), BF16), vm((768, 1536), BF16), vm((384, 768), BF16), vm((1536, 768), BF16),
        vm((8, 512), F32), vm((4, 8, 512), F32), vm((8, 512), F32),
        vm((8, 2, 32, 384), F32), vm((3, 2, 2, 32, 384), F32),
        vm((2, 2, 32, 384), F32), vm((2, 2, 32, 384), F32),
        vm((2, 8, 2, 32, 768), F32), vm((2, 8, 2, 32, 768), BF16),
        vm((2, 2, 3, 2, 32, 768), BF16), vm((2, 2, 2, 32, 768), F32),
        vm((2, 2, 2, 32, 768), BF16), vm((2, 2, 2, 32, 768), BF16),
        vm((8, 2, 32, 384), BF16), vm((2, 2, 8, 2, 32, 768), BF16), vm((2, 3, 512, 384), BF16),
        vm((4, 8, 2, 32, 384), BF16), vm((2, 8, 2, 32, 384), BF16), vm((2, 512, 384), BF16),
        vm((768, 512), BF16), vm((2, 192, 1024), BF16),
        vm((6, 256, 256), F32), vm((512, 384), BF16), vm((512, 384), BF16),
        vm((8, 2, 32, 768), F32), vm((2, 8, 32, 768), BF16), vm((2, 7, 32, 768), BF16),
        vm((8, 128), F32), vm((4, 8, 128), F32), vm((8, 128), F32),
        vm((2, 384, 768), F32), vm((384, 768), F32), vm((2, 3, 192, 384), F32),
        vm((2, 2, 192, 768), F32),
        vm((384, 768), BF16), vm((384, 768), BF16), vm((96, 768), BF16), vm((96, 768), BF16),
        vm((3, 192, 384), BF16), vm((3, 192, 384), BF16),
        vm((2, 192, 768), BF16), vm((2, 192, 768), BF16),
        pltpu.SemaphoreType.DMA((10,)),
        pltpu.SemaphoreType.DMA((N_COPIES,)),
        pltpu.SemaphoreType.DMA((N_COPIES,)),
    ]
    results = pl.pallas_call(
        kernel,
        out_shape=(
            jax.ShapeDtypeStruct((64, 768), BF16),
            jax.ShapeDtypeStruct((3, 192, 384), BF16),
            jax.ShapeDtypeStruct((192, 1536), BF16),
            jax.ShapeDtypeStruct((96, 768), BF16),
            jax.ShapeDtypeStruct((384, 768), BF16),
        ),
        in_specs=[pl.BlockSpec(memory_space=pl.ANY)] * 8,
        out_specs=[pl.BlockSpec(memory_space=pltpu.VMEM)] * 5,
        scratch_shapes=scratch,
        compiler_params=pltpu.CompilerParams(
            collective_id=0, has_side_effects=True, vmem_limit_bytes=58 * 2**20
        ),
        name="layer_backward",
    )(
        inputs.reshape(8, 2, 32, 768),
        saved_qkv.transpose(1, 0, 2),
        saved_up.reshape(8, 2, 32, 1536),
        cotangent.reshape(8, 2, 32, 768),
        weight_qkv.transpose(1, 0, 2),
        weight_up,
        weight_attn,
        weight_down,
    )
    gin, gqkv, gup, gattn, gdown = pl.pallas_call(
        hand_over,
        out_shape=tuple(jax.ShapeDtypeStruct(r.shape, r.dtype) for r in results),
        in_specs=[pl.BlockSpec(memory_space=pl.ANY)] * 5,
        out_specs=[pl.BlockSpec(memory_space=pl.ANY)] * 5,
        scratch_shapes=[vm(r.shape, r.dtype) for r in results] + [pltpu.SemaphoreType.DMA((10,))],
        name="hand_over",
    )(*results)
    return (
        gin,
        gqkv.transpose(1, 0, 2).reshape(1, 1, 192, 3, 384),
        gup.reshape(1, 1, 192, 1536),
        gattn.reshape(1, 1, 96, 768),
        gdown.reshape(1, 1, 384, 768),
    )


def solution(mesh):
    return jax.shard_map(
        body,
        mesh=mesh,
        in_specs=(
            P("dp", "row"),
            P("dp", None, "col"),
            P("dp", "col"),
            P("dp", "row"),
            P("row", None, "col"),
            P("row", "col"),
            P("col", "row"),
            P("col", "row"),
        ),
        out_specs=(
            P(("dp", "col"), "row"),
            P("row", "dp", None, None, "col"),
            P("row", "dp", None, "col"),
            P("col", "dp", None, "row"),
            P("col", "dp", None, "row"),
        ),
        check_vma=False,
    )
```

```python
import jax
import jax.numpy as jnp
from jax import lax
from jax.experimental import pallas as pl
from jax.experimental.pallas import tpu as pltpu
from jax.sharding import PartitionSpec as P

MESH = pl.DeviceIdType.MESH
HD = 128
S = 256
EPS = 1e-06
SQRT_HALF = 0.7071067811865476
INV_ROOT_TWO_PI = 0.3989422804014327
F32 = jnp.float32
BF16 = jnp.bfloat16
N_COPIES = 86


def nt(a, b):
    return lax.dot_general(a, b, (((1,), (1,)), ((), ())), preferred_element_type=F32)


def tn(a, b):
    return lax.dot_general(a, b, (((0,), (0,)), ((), ())), preferred_element_type=F32)


def nn(a, b):
    return lax.dot_general(a, b, (((1,), (0,)), ((), ())), preferred_element_type=F32)


def gelu_exact(values):
    return 0.5 * values * (1.0 + lax.erf(values * SQRT_HALF))


def gelu_slope(values):
    cumul = 0.5 * (1.0 + lax.erf(values * SQRT_HALF))
    return cumul + values * jnp.exp(-0.5 * values * values) * INV_ROOT_TWO_PI


def head_norm(values):
    average = jnp.mean(values, axis=-1, keepdims=True)
    centred = values - average
    inv_std = lax.rsqrt(jnp.mean(centred * centred, axis=-1, keepdims=True) + EPS)
    return (centred * inv_std, inv_std)


def head_norm_back(normed, inv_std, upstream):
    first = jnp.mean(upstream, axis=-1, keepdims=True)
    cross = jnp.mean(upstream * normed, axis=-1, keepdims=True)
    return inv_std * (upstream - first - normed * cross)


def span(start, size):
    return pl.ds(pl.multiple_of(start, size), size)


def kernel(
    inp_h, qkv_h, up_h, cot_h, wqkv_h, wup_h, wattn_h, wdown_h,
    gin_o, gqkv_o, gup_o, gattn_o, gdown_o,
    inp, qkv, up, cot, wqkv, wup, wattn, wdown,
    stat_s, stat_r, stat_y,
    pa, pa_r, pay_s, pay_r,
    ph, phb, ph_r, phx, phw_r, phy_s, phy_r,
    go, gp, gf, hid, hid_s, att, n_t, n_p, probs_v, qn_v, kn_v,
    tot, zs, zr, fin_s, fin_r, fin_y,
    wgd, wga, wgq, wgu, ysd, yrd, ysa, yra, ysq, yrq, ysu, yru,
    load_sem, send_sem, recv_sem,
):
    dp, row, col = lax.axis_index("dp"), lax.axis_index("row"), lax.axis_index("col")
    y_lo, core = dp // 2, dp % 2
    x, y_hi = row // 2, row % 2
    y_other = 1 - y_lo
    width = 6144.0
    scale = HD ** (-0.5)
    x_next, x_far, x_prev = (x + 1) % 4, (x + 2) % 4, (x + 3) % 4
    sib_dev = (y_lo * 2 + (1 - core), row, col)
    ylo_dev = (y_other * 2 + core, row, col)
    yhi_dev = (dp, x * 2 + (1 - y_hi), col)
    next_dev = (dp, x_next * 2 + y_hi, col)
    far_dev = (dp, x_far * 2 + y_hi, col)
    prev_dev = (dp, x_prev * 2 + y_hi, col)
    x_dev = [next_dev, far_dev, prev_dev]
    z_of = [(col + d) % 8 for d in range(1, 8)]
    z_dev = [(dp, row, zp) for zp in z_of]

    def load(i, src, dst):
        cp = pltpu.make_async_copy(src, dst, load_sem.at[i])
        cp.start()
        return cp

    l_cot = load(0, cot_h, cot.at[0])
    l_wattn = load(1, wattn_h, wattn)

    partners = [sib_dev, ylo_dev, yhi_dev] + x_dev + z_dev
    barrier = pltpu.get_barrier_semaphore()
    for dev in partners:
        pl.semaphore_signal(barrier, inc=1, device_id=dev, device_id_type=MESH)

    sent = []

    def push(src, dst, dev):
        i = len(sent)
        cp = pltpu.make_async_remote_copy(
            src, dst, send_sem.at[i], recv_sem.at[i], device_id=dev, device_id_type=MESH
        )
        cp.start()
        sent.append(cp)
        return cp

    x_of = [x_next, x_far, x_prev]

    def scatter(block, land):
        return [push(block(x_of[d]), land.at[d], x_dev[d]) for d in range(3)]

    def gather(chunk):
        cps = []
        for dev in (next_dev, prev_dev):
            for i in range(2):
                ref = chunk(2 * x + i)
                cps.append(push(ref, ref, dev))
        return cps

    def gather_far(chunk, cps):
        cps[0].wait_recv()
        ref = chunk(2 * x_prev)
        cps.append(push(ref, ref, next_dev))
        cps[3].wait_recv()
        ref = chunk(2 * x_next + 1)
        cps.append(push(ref, ref, prev_dev))

    def gather_end(cps):
        for i in (1, 2, 4, 5):
            cps[i].wait_recv()

    l_cot.wait()
    l_wattn.wait()

    @pl.loop(0, 2)
    def _(b):
        acc = nt(cot[0, pl.ds(b * 4, 4)].reshape(256, 768), wattn[...])
        pa[pl.ds(b * 4, 4)] = acc.reshape(4, 2, 32, 384)

    l_up = load(2, up_h, up)
    l_wdown = load(3, wdown_h, wdown)
    l_qkv = load(4, qkv_h, qkv)
    l_inp = load(5, inp_h, inp)

    def activate(y):
        @pl.loop(0, 16)
        def _(i):
            r, s = i // 2, 2 * y + i % 2
            hid[s, r] = gelu_exact(up[r, :, :, span(s * 384, 384)].astype(F32)).astype(BF16)

    pl.semaphore_wait(barrier, len(partners))
    c_pa = scatter(lambda xp: pa.at[pl.ds(2 * xp, 2)], pa_r)
    c_cot = push(cot.at[0], cot.at[1], sib_dev)
    l_up.wait()
    activate(y_other)
    c_hid = [push(hid.at[2 * y_other + 1 - core], hid_s.at[y_other], sib_dev)]
    l_wdown.wait()
    l_wqkv = load(6, wqkv_h, wqkv)
    l_wup = load(7, wup_h, wup)

    def hidden_start(c, p):
        @pl.loop(0, 3)
        def _(n):
            cols = span(n * 256, 256)
            acc = nt(
                cot[0, :, p].reshape(256, 768), wdown[span(c * 768 + n * 256, 256), :]
            ).reshape(8, 32, 256)
            ph[c, :, p, :, cols] = acc
            phb[c, :, p, :, cols] = acc.astype(BF16)

        return scatter(lambda xp: phb.at[c, pl.ds(2 * xp, 2), p], ph_r.at[c, p])

    def hidden_sum(c, p, cps):
        for cp in cps:
            cp.wait_recv()
        total = ph[c, pl.ds(2 * x, 2), p]
        for d in range(3):
            total = total + ph_r[c, p, d].astype(F32)
        phx[c, p] = total
        if c == 0:
            return push(phx.at[c, p], phw_r.at[p], yhi_dev)
        phy_s[p] = total.astype(BF16)
        return push(phy_s.at[p], phy_r.at[p], yhi_dev)

    def hidden_chunk(c, p):
        return lambda r: gp.at[0, c, r, p]

    def hidden_slope(c, p, cp):
        slope = gelu_slope(up[pl.ds(2 * x, 2), p, :, c * 768 : (c + 1) * 768].astype(F32))
        cp.wait_recv()
        gp[0, c, pl.ds(2 * x, 2), p] = (
            (phx[c, p] + (phw_r[p] if c == 0 else phy_r[p].astype(F32))) * slope
        ).astype(BF16)
        return gather(hidden_chunk(c, p))

    def down(j):
        @pl.loop(0, 3)
        def _(n):
            cols = span(n * 256, 256)
            acc = tn(hid[2 * j + core].reshape(512, 384), cot[0, :, :, :, cols].reshape(512, 256))
            acc += tn(hid_s[j].reshape(512, 384), cot[1, :, :, :, cols].reshape(512, 256))
            wgd[j, :, cols] = acc

    def attention(b):
        @pl.loop(0, 3)
        def _(h):
            rows = pl.ds(b * 256, 256)
            lanes = span(h * 128, 128)
            qn, _ = head_norm(qkv[0, rows, lanes].astype(F32))
            kn, _ = head_norm(qkv[1, rows, lanes].astype(F32))
            qn_b = qn.astype(BF16)
            kn_b = kn.astype(BF16)
            qn_v[rows, lanes] = qn_b
            kn_v[rows, lanes] = kn_b
            expo = jnp.exp(nt(qn_b, kn_b) * scale)
            probs = expo / jnp.sum(expo, axis=-1, keepdims=True)
            probs_v[b * 3 + h] = probs
            att[0, rows, lanes] = nn(probs.astype(BF16), qkv[2, rows, lanes]).astype(BF16)

    def attention_back(b):
        @pl.loop(0, 3)
        def _(h):
            rows = pl.ds(b * 256, 256)
            lanes = span(h * 128, 128)
            grad_o = go[pl.ds(b * 4, 4), :, :, lanes].reshape(256, 128)
            probs = probs_v[b * 3 + h]
            probs_b = probs.astype(BF16)
            grad_probs = nt(grad_o, qkv[2, rows, lanes])
            gf[0, 2, rows, lanes] = tn(probs_b, grad_o).astype(BF16)
            rowdot = jnp.sum(probs * grad_probs, axis=-1, keepdims=True)
            grad_scores = (probs * (grad_probs - rowdot) * scale).astype(BF16)
            q_norm, q_inv = head_norm(qkv[0, rows, lanes].astype(F32))
            grad_qn = nn(grad_scores, kn_v[rows, lanes])
            gf[0, 0, rows, lanes] = head_norm_back(q_norm, q_inv, grad_qn).astype(BF16)
            k_norm, k_inv = head_norm(qkv[1, rows, lanes].astype(F32))
            grad_kn = tn(grad_scores, qn_v[rows, lanes])
            gf[0, 1, rows, lanes] = head_norm_back(k_norm, k_inv, grad_kn).astype(BF16)

    def share(c, p):
        gather_end(c_gp[c, p])
        return push(gp.at[0, c, :, p], gp.at[1, c, :, p], sib_dev)

    c_ph = {}
    c_ph[0, 0] = hidden_start(0, 0)

    c_cot.wait_recv()
    c_hid[0].wait_recv()
    down(y_other)
    ysd[...] = wgd[y_other].astype(BF16)
    c_d = [push(ysd.at[0:192], yrd.at[0:192], ylo_dev)]

    c_ph[0, 1] = hidden_start(0, 1)
    c_ph[1, 0] = hidden_start(1, 0)
    c_ph[1, 1] = hidden_start(1, 1)

    l_qkv.wait()
    attention(0)

    mine = pl.ds(2 * x, 2)
    for cp in c_pa:
        cp.wait_recv()
    pay_s[...] = pa[mine] + pa_r[0] + pa_r[1] + pa_r[2]
    c_pay = push(pay_s, pay_r, yhi_dev)

    attention(1)
    c_att = push(att.at[0], att.at[1], sib_dev)

    l_inp.wait()
    stat_s[...] = jnp.zeros_like(stat_s)
    for g in range(4):
        block_t = inp[2 * g : 2 * g + 2].reshape(128, 768).astype(F32).T
        lanes = pl.ds(g * 128, 128)
        stat_s[0:1, lanes] = jnp.sum(block_t, axis=0, keepdims=True)
        stat_s[1:2, lanes] = jnp.sum(block_t * block_t, axis=0, keepdims=True)
        n_t[:, lanes] = block_t.astype(BF16)
    c_stat = [push(stat_s, stat_r.at[d], x_dev[d]) for d in range(3)]

    c_att.wait_recv()

    @pl.loop(0, 3)
    def _(n):
        cols = span(n * 256, 256)
        acc = tn(att[0], cot[0, :, :, :, cols].reshape(512, 256))
        acc += tn(att[1], cot[1, :, :, :, cols].reshape(512, 256))
        wga[:, cols] = acc

    ysa[...] = wga[span((2 * y_other + core) * 96, 96), :].astype(BF16)

    activate(y_lo)
    c_hid.append(push(hid.at[2 * y_lo + 1 - core], hid_s.at[y_lo], sib_dev))
    c_pay.wait_recv()
    go[mine] = (pay_s[...] + pay_r[...]).astype(BF16)
    c_go = [push(go.at[mine], go.at[mine], dev) for dev in x_dev]
    c_hid[1].wait_recv()
    down(y_lo)
    c_phy = {(0, 0): hidden_sum(0, 0, c_ph[0, 0])}
    c_phy[0, 1] = hidden_sum(0, 1, c_ph[0, 1])

    for cp in c_stat:
        cp.wait_recv()
    stat_y[...] = stat_s[...] + stat_r[0] + stat_r[1] + stat_r[2]
    c_staty = push(stat_y, stat_r.at[3], yhi_dev)

    c_gp = {(0, 0): hidden_slope(0, 0, c_phy[0, 0])}
    c_phy[1, 0] = hidden_sum(1, 0, c_ph[1, 0])
    c_gp[0, 1] = hidden_slope(0, 1, c_phy[0, 1])
    c_phy[1, 1] = hidden_sum(1, 1, c_ph[1, 1])
    c_d.append(push(ysd.at[192:384], yrd.at[192:384], ylo_dev))
    c_a = push(ysa, yra, ylo_dev)

    c_staty.wait_recv()
    stat = stat_y[...] + stat_r[3]
    mean_r = stat[0:1] / width
    inv_r = lax.rsqrt(stat[1:2] / width - mean_r * mean_r + EPS)

    @pl.loop(0, 8)
    def _(k):
        rows = span(k * 96, 96)
        n_t[rows, :] = ((n_t[rows, :].astype(F32) - mean_r) * inv_r).astype(BF16)

    c_nt = [
        push(n_t.at[span((2 * j + 1 - core) * 192, 192)], n_p.at[j, :, pl.ds(512, 512)], sib_dev)
        for j in range(2)
    ]
    l_nt = []
    for j in range(2):
        cp = pltpu.make_async_copy(
            n_t.at[span((2 * j + core) * 192, 192)], n_p.at[j, :, pl.ds(0, 512)], load_sem.at[8 + j]
        )
        cp.start()
        l_nt.append(cp)

    for cp in c_go:
        cp.wait_recv()
    attention_back(0)
    c_gp[1, 0] = hidden_slope(1, 0, c_phy[1, 0])
    attention_back(1)
    c_gf = push(gf.at[0], gf.at[1], sib_dev)
    c_gp[1, 1] = hidden_slope(1, 1, c_phy[1, 1])
    gather_far(hidden_chunk(0, 0), c_gp[0, 0])
    gather_far(hidden_chunk(0, 1), c_gp[0, 1])
    for cp in c_nt:
        cp.wait_recv()
    for cp in l_nt:
        cp.wait()

    c_gf.wait_recv()

    @pl.loop(0, 3)
    def _(n):
        acc = nn(n_p[...].reshape(384, 1024), gf[:, n].reshape(1024, 384))
        wgq[:, n] = acc.reshape(2, 192, 384)

    ysq[...] = wgq[y_other].astype(BF16)
    c_q = push(ysq, yrq, ylo_dev)

    gather_far(hidden_chunk(1, 0), c_gp[1, 0])
    gather_far(hidden_chunk(1, 1), c_gp[1, 1])
    c_gps = [share(0, 0), share(0, 1)]

    l_wqkv.wait()
    l_wup.wait()

    @pl.loop(0, 6)
    def _(i):
        b, n = i // 3, i % 3
        cols = span(n * 256, 256)
        rows = span(b * 256, 256)
        acc = nt(gf[0, 0, rows, :], wqkv[0, cols, :])
        acc += nt(gf[0, 1, rows, :], wqkv[1, cols, :])
        acc += nt(gf[0, 2, rows, :], wqkv[2, cols, :])
        tot[pl.ds(b * 4, 4), :, :, cols] = acc.reshape(4, 2, 32, 256)

    def grad_up(c):
        @pl.loop(0, 3)
        def _(n):
            cols = span(n * 256, 256)
            acc = nn(n_p[...].reshape(384, 1024), gp[:, c, :, :, :, cols].reshape(1024, 256))
            wgu[c, :, :, cols] = acc.reshape(2, 192, 256)

        ysu[c] = wgu[c, y_other].astype(BF16)
        return push(ysu.at[c], yru.at[c], ylo_dev)

    for cp in c_gps:
        cp.wait_recv()
    c_u = [grad_up(0)]

    c_z = []
    c_gps = []
    for p in range(2):
        c_gps.append(share(1, p))

        @pl.loop(0, 3)
        def _(n):
            cols = span(n * 256, 256)
            acc = nt(gp[0, 0, :, p].reshape(256, 768), wup[cols, 0:768])
            acc += nt(gp[0, 1, :, p].reshape(256, 768), wup[cols, 768:1536])
            acc = acc.reshape(8, 32, 256) + tot[:, p, :, cols]
            tot[:, p, :, cols] = acc
            zs[p, :, :, cols] = acc.astype(BF16)

        c_z.append([push(zs.at[p, z_of[d]], zr.at[p, d], z_dev[d]) for d in range(7)])

    for cp in c_gps:
        cp.wait_recv()
    c_u.append(grad_up(1))
    lane = lax.broadcasted_iota(jnp.int32, (64, 512), 1)
    token = lax.broadcasted_iota(jnp.int32, (64, 512), 0)
    pick = jnp.where(lane == token + col * 64, 1.0, 0.0).astype(F32)
    mean_c = jnp.sum(pick * mean_r, axis=1, keepdims=True)
    inv_c = jnp.sum(pick * inv_r, axis=1, keepdims=True)
    normed = (inp[col].reshape(64, 768).astype(F32) - mean_c) * inv_c
    gn = []
    for p in range(2):
        for cp in c_z[p]:
            cp.wait_recv()
        value = tot[col, p]
        for d in range(7):
            value = value + zr[p, d].astype(F32)
        gn.append(value)
    grad_n = jnp.concatenate(gn, axis=0)
    sum_g = jnp.sum(grad_n, axis=1, keepdims=True)
    sum_c = jnp.sum(grad_n * normed, axis=1, keepdims=True)
    lane = lax.broadcasted_iota(jnp.int32, (64, 128), 1)
    token = lax.broadcasted_iota(jnp.int32, (64, 128), 0)
    eye = jnp.where(lane == token, 1.0, 0.0).astype(F32)
    fin_s[...] = jnp.zeros_like(fin_s)
    fin_s[0:1, :] = jnp.sum(eye * sum_g, axis=0, keepdims=True)
    fin_s[1:2, :] = jnp.sum(eye * sum_c, axis=0, keepdims=True)
    c_fin = [push(fin_s, fin_r.at[d], x_dev[d]) for d in range(3)]

    for cp in c_d:
        cp.wait_recv()
    gdown_o[...] = (wgd[y_lo] + yrd[...].astype(F32)).astype(BF16)
    c_a.wait_recv()
    gattn_o[...] = (
        wga[span((2 * y_lo + core) * 96, 96), :] + yra[...].astype(F32)
    ).astype(BF16)

    for cp in c_fin:
        cp.wait_recv()
    fin_y[...] = fin_s[...] + fin_r[0] + fin_r[1] + fin_r[2]
    c_finy = push(fin_y, fin_r.at[3], yhi_dev)

    c_q.wait_recv()
    gqkv_o[...] = (wgq[y_lo] + yrq[...].astype(F32)).astype(BF16)

    c_finy.wait_recv()
    fin = fin_y[...] + fin_r[3]
    mean_g = jnp.sum(eye * fin[0:1], axis=1, keepdims=True) / width
    mean_x = jnp.sum(eye * fin[1:2], axis=1, keepdims=True) / width
    branch = grad_n - mean_g - normed * mean_x
    result = cot[0, col].reshape(64, 768).astype(F32) + inv_c * branch
    gin_o[...] = result.astype(BF16)

    for c in range(2):
        c_u[c].wait_recv()
        gup_o[:, c * 768 : (c + 1) * 768] = (
            wgu[c, y_lo] + yru[c].astype(F32)
        ).astype(BF16)

    for cp in sent:
        cp.wait_send()
    assert len(sent) == N_COPIES, len(sent)


def hand_over(*refs):
    sem = refs[15]
    copies_in = [pltpu.make_async_copy(refs[i], refs[10 + i], sem.at[i]) for i in range(5)]
    copies_out = [pltpu.make_async_copy(refs[10 + i], refs[5 + i], sem.at[5 + i]) for i in range(5)]
    for cp in copies_in:
        cp.start()
    for first, second in zip(copies_in, copies_out):
        first.wait()
        second.start()
    for cp in copies_out:
        cp.wait()


def body(inputs, saved_qkv, saved_up, cotangent, weight_qkv, weight_up, weight_attn, weight_down):
    vm = pltpu.VMEM
    scratch = [
        vm((8, 2, 32, 768), BF16), vm((3, 512, 384), BF16), vm((8, 2, 32, 1536), BF16),
        vm((2, 8, 2, 32, 768), BF16),
        vm((3, 768, 384), BF16), vm((768, 1536), BF16), vm((384, 768), BF16), vm((1536, 768), BF16),
        vm((8, 512), F32), vm((4, 8, 512), F32), vm((8, 512), F32),
        vm((8, 2, 32, 384), F32), vm((3, 2, 2, 32, 384), F32),
        vm((2, 2, 32, 384), F32), vm((2, 2, 32, 384), F32),
        vm((2, 8, 2, 32, 768), F32), vm((2, 8, 2, 32, 768), BF16),
        vm((2, 2, 3, 2, 32, 768), BF16), vm((2, 2, 2, 32, 768), F32),
        vm((2, 2, 32, 768), F32), vm((2, 2, 32, 768), BF16), vm((2, 2, 32, 768), BF16),
        vm((8, 2, 32, 384), BF16), vm((2, 2, 8, 2, 32, 768), BF16), vm((2, 3, 512, 384), BF16),
        vm((4, 8, 2, 32, 384), BF16), vm((2, 8, 2, 32, 384), BF16), vm((2, 512, 384), BF16),
        vm((768, 512), BF16), vm((2, 192, 1024), BF16),
        vm((6, 256, 256), F32), vm((512, 384), BF16), vm((512, 384), BF16),
        vm((8, 2, 32, 768), F32), vm((2, 8, 32, 768), BF16), vm((2, 7, 32, 768), BF16),
        vm((8, 128), F32), vm((4, 8, 128), F32), vm((8, 128), F32),
        vm((2, 384, 768), F32), vm((384, 768), F32), vm((2, 3, 192, 384), F32),
        vm((2, 2, 192, 768), F32),
        vm((384, 768), BF16), vm((384, 768), BF16), vm((96, 768), BF16), vm((96, 768), BF16),
        vm((3, 192, 384), BF16), vm((3, 192, 384), BF16),
        vm((2, 192, 768), BF16), vm((2, 192, 768), BF16),
        pltpu.SemaphoreType.DMA((10,)),
        pltpu.SemaphoreType.DMA((N_COPIES,)),
        pltpu.SemaphoreType.DMA((N_COPIES,)),
    ]
    results = pl.pallas_call(
        kernel,
        out_shape=(
            jax.ShapeDtypeStruct((64, 768), BF16),
            jax.ShapeDtypeStruct((3, 192, 384), BF16),
            jax.ShapeDtypeStruct((192, 1536), BF16),
            jax.ShapeDtypeStruct((96, 768), BF16),
            jax.ShapeDtypeStruct((384, 768), BF16),
        ),
        in_specs=[pl.BlockSpec(memory_space=pl.ANY)] * 8,
        out_specs=[pl.BlockSpec(memory_space=pltpu.VMEM)] * 5,
        scratch_shapes=scratch,
        compiler_params=pltpu.CompilerParams(
            collective_id=0, has_side_effects=True, vmem_limit_bytes=58 * 2**20
        ),
        name="layer_backward",
    )(
        inputs.reshape(8, 2, 32, 768),
        saved_qkv.transpose(1, 0, 2),
        saved_up.reshape(8, 2, 32, 1536),
        cotangent.reshape(8, 2, 32, 768),
        weight_qkv.transpose(1, 0, 2),
        weight_up,
        weight_attn,
        weight_down,
    )
    gin, gqkv, gup, gattn, gdown = pl.pallas_call(
        hand_over,
        out_shape=tuple(jax.ShapeDtypeStruct(r.shape, r.dtype) for r in results),
        in_specs=[pl.BlockSpec(memory_space=pl.ANY)] * 5,
        out_specs=[pl.BlockSpec(memory_space=pl.ANY)] * 5,
        scratch_shapes=[vm(r.shape, r.dtype) for r in results] + [pltpu.SemaphoreType.DMA((10,))],
        name="hand_over",
    )(*results)
    return (
        gin,
        gqkv.transpose(1, 0, 2).reshape(1, 1, 192, 3, 384),
        gup.reshape(1, 1, 192, 1536),
        gattn.reshape(1, 1, 96, 768),
        gdown.reshape(1, 1, 384, 768),
    )


def solution(mesh):
    return jax.shard_map(
        body,
        mesh=mesh,
        in_specs=(
            P("dp", "row"),
            P("dp", None, "col"),
            P("dp", "col"),
            P("dp", "row"),
            P("row", None, "col"),
            P("row", "col"),
            P("col", "row"),
            P("col", "row"),
        ),
        out_specs=(
            P(("dp", "col"), "row"),
            P("row", "dp", None, None, "col"),
            P("row", "dp", None, "col"),
            P("col", "dp", None, "row"),
            P("col", "dp", None, "row"),
        ),
        check_vma=False,
    )
```
